256 devices in a mesh: cuts: 16 (over y_lo, z), fsdp: 16 (over x, y_hi, core).
Axes of the slice: x: 4, y: 4 (y_hi: 2, y_lo: 2; y = y_hi * 2 + y_lo), z: 8, core: 2. Of those that a mesh axis runs over, the one named last changes fastest.
Arguments:
- tokens: bfloat16 [32768, 2560], P(('cuts', 'fsdp')), may hold values from -6 to 6
- upstream: bfloat16 [32768, 6912], P(('cuts', 'fsdp')), may hold values from -24 to 24
- gate_weight: bfloat16 [2560, 6912], P(None, 'fsdp'), may hold values from -0.125 to 0.125
- probe: bfloat16 [2560, 6912], P(None, 'fsdp'), may hold values from -6 to 6
Outputs:
- curvature: float32 [2560, 6912], P(None, 'fsdp')
The draws below stay inside these ranges and needn't reach their ends.
All inputs are finite; a program needn't handle non-finite values.
Results may differ from the reference program's by a relative error of at most 0.0029.
Values may be sent and summed in bfloat16 or wider, within the bound.
No kernel may reach another device: no remote copies, remote signals or barrier semaphores. Data moves between devices by JAX's collectives and lax.ppermute only.
A program may use at most 128 MiB of HBM per device.

```python
import jax
import jax.numpy as jnp
from jax import lax

D = 2560
FFW = 6912
TOK_DEV = 128
TOKENS = 32768
N_CUTS = 16
N_FSDP = 16


def block_scale(stream_key, extent, pieces, least, largest):
    loudness, own = 1.0, jax.random.fold_in(stream_key, 6)
    for axis_at, parts in pieces:
        draws = jnp.exp(jax.random.uniform(jax.random.fold_in(own, axis_at), (parts,), jnp.float32, least / len(pieces), largest / len(pieces)))
        loudness = loudness * jnp.repeat(draws, extent[axis_at] // parts).reshape([-1 if axis == axis_at else 1 for axis in range(len(extent))])
    return loudness


def bell_draw(rng, dims, scale, most, shards=(), held_as=jnp.bfloat16):
    entries = scale * jax.random.normal(rng, dims, jnp.float32)
    if shards:
        entries = entries * block_scale(rng, dims, shards, -0.22, 0.18)
    return jnp.clip(entries, -most, most).astype(held_as)


def setup_inputs(seed: int = 0) -> dict:
    seeds = jax.random.split(jax.random.key(seed), 5)
    return {
        "tokens": bell_draw(seeds[0], (TOKENS, D), 1.0, 6.0, ((0, 256),)),
        "upstream": bell_draw(seeds[1], (TOKENS, FFW), 4.0, 24.0, ((0, 256),)),
        "gate_weight": bell_draw(seeds[2], (D, FFW), D ** -0.5, 0.125, ((1, 16),)),
        "probe": bell_draw(seeds[3], (D, FFW), 1.0, 6.0, ((1, 16),)),
    }


def reference(tokens, upstream, gate_weight, probe):
    replica_rows = TOK_DEV * N_FSDP
    token_blocks = tokens.reshape(N_CUTS, replica_rows, D)
    grad_blocks = upstream.reshape(N_CUTS, replica_rows, FFW)

    def accumulate(running, blocks):
        token_block, grad_block = blocks
        gate_out = jnp.dot(token_block, gate_weight, preferred_element_type=jnp.float32)
        tangent = jnp.dot(token_block, probe, preferred_element_type=jnp.float32)
        logistic = jax.nn.sigmoid(gate_out)
        bend_factor = logistic * (1.0 - logistic) * (2.0 + gate_out * (1.0 - 2.0 * logistic))
        weighted = (grad_block.astype(jnp.float32) * bend_factor * tangent).astype(jnp.bfloat16)
        product = lax.dot_general(token_block, weighted, (((0,), (0,)), ((), ())), preferred_element_type=jnp.float32)
        return running + product, None

    summed, _ = lax.scan(accumulate, jnp.zeros((D, FFW), jnp.float32), (token_blocks, grad_blocks))
    hvp = summed / TOKENS
    return probe.astype(jnp.float32) * hvp
```

```python
import jax
import jax.numpy as jnp
from jax import lax
from jax.experimental import pallas as pl
from jax.experimental.pallas import tpu as pltpu
from jax.sharding import PartitionSpec as P

AXES = ("cuts", "fsdp")
NX, NY, NZ, NC = 4, 4, 8, 2
F32, BF16 = jnp.float32, jnp.bfloat16
VMEM_LIMIT = 62_000_000

PIECE = 56


def device(x, y, z, core):
    return ((y % 2) * NZ + z) * (NX * 2 * NC) + (x * 2 + y // 2) * NC + core


def moves(step):
    chips = [(x, y, z, c) for x in range(NX) for y in range(NY) for z in range(NZ) for c in range(NC)]
    return [(device(*at), device(*step(*at))) for at in chips]


X_UP = moves(lambda x, y, z, c: ((x + 1) % NX, y, z, c))
X_DOWN = moves(lambda x, y, z, c: ((x - 1) % NX, y, z, c))
Z_UP = moves(lambda x, y, z, c: (x, y, (z + 1) % NZ, c))
Z_DOWN = moves(lambda x, y, z, c: (x, y, (z - 1) % NZ, c))
Y_MATE = moves(lambda x, y, z, c: (x, 3 - y, z, c))
Y_CUT = moves(lambda x, y, z, c: (x, y ^ 1, z, c))
CORE = moves(lambda x, y, z, c: (x, y, z, 1 - c))

REPLICAS = [
    [device(x, (low, 3 - low)[high], z, c) for x in range(NX) for high in range(2) for c in range(NC)]
    for low in range(2)
    for z in range(NZ)
]
Z_RINGS = [
    [device(x, y, z, c) for z in range(NZ)] for x in range(NX) for y in range(NY) for c in range(NC)
]


def send(value, pairs):
    return lax.ppermute(value, AXES, pairs)


def after(values, *before):
    return lax.optimization_barrier((*values, *before))[: len(values)]


def params():
    return pltpu.CompilerParams(vmem_limit_bytes=VMEM_LIMIT)


def factor_kernel(weighing, table_ref, gate_ref, probe_ref, *refs):
    tokens_ref, out_ref = refs[-1], refs[-2]
    grads, groups = (refs[:2], refs[2:-2]) if weighing else ((), refs[:-2])
    n = out_ref.shape[2]

    def take(mine_ref, core_ref):
        tokens_ref[:n] = mine_ref[...]
        tokens_ref[n:] = core_ref[...]

    if len(groups) == 2:
        take(*groups)
    else:
        pl.when(pl.program_id(0) == 0)(lambda: take(*groups[:2]))
        pl.when(pl.program_id(0) > 0)(lambda: take(*groups[2:]))
    across = (((1,), (1,)), ((), ()))
    gate = lax.dot_general(gate_ref[...], tokens_ref[...], across, preferred_element_type=F32)
    tangent = lax.dot_general(probe_ref[...], tokens_ref[...], across, preferred_element_type=F32)
    s = 1.0 / (1.0 + jnp.exp(-gate))
    bend = s * (1.0 - s) * (2.0 + gate * (1.0 - 2.0 * s))
    for side in range(2):
        at = slice(side * n, side * n + n)
        if weighing:
            out_ref[side] = (grads[side][0].astype(F32) * bend[:, at] * tangent[:, at]).astype(BF16)
        else:
            out_ref[side] = bend[:, at] * tangent[:, at]


def factor(table, first, gate_t, probe_t, spread, *tokens):
    hidden, depth = gate_t.shape
    rows = 128
    total = sum(t.shape[0] for t in tokens[::2])
    later = int(len(tokens) == 4)
    block = lambda skip: pl.BlockSpec((rows, depth), lambda j, o: (jnp.maximum(j - skip, 0), 0))
    only = pl.BlockSpec((rows, depth), lambda j, o: (0, 0))
    weighing = spread is not None
    return pl.pallas_call(
        lambda *refs: factor_kernel(weighing, *refs),
        grid_spec=pltpu.PrefetchScalarGridSpec(
            num_scalar_prefetch=1,
            grid=(total // rows,),
            in_specs=[pl.BlockSpec((hidden, depth), lambda j, o: (0, 0))] * 2
            + [
                pl.BlockSpec((1, hidden, rows), lambda j, o, side=side: (o[first + 2 * j + side], 0, 0))
                for side in range(2)
            ]
            * weighing
            + [only, only] * later
            + [block(later), block(later)],
            out_specs=pl.BlockSpec((2, hidden, rows), lambda j, o: (0, 0, j)),
            scratch_shapes=[pltpu.VMEM((2 * rows, depth), BF16)],
        ),
        out_shape=jax.ShapeDtypeStruct((2, hidden, total), BF16 if weighing else F32),
        compiler_params=params(),
        cost_estimate=pl.CostEstimate(flops=0, bytes_accessed=0, transcendentals=0),
        name="factor",
    )(table, gate_t, probe_t, *[spread, spread] * weighing, *tokens)


def weigh_kernel(table_ref, grad_ref, *refs):
    factor_refs, out_ref = refs[:-1], refs[-1]
    for side in range(2):
        at = 0
        for factor_ref in factor_refs:
            for k in range(0, factor_ref.shape[2], 128):
                grad = grad_ref[table_ref[2 * at + side]].astype(F32)
                to = (side * 8 + at) * 128
                out_ref[:, to : to + 128] = (grad * factor_ref[side, :, k : k + 128]).astype(BF16)
                at += 1


def weigh(table, spread, factors):
    _, hidden, _ = factors[0].shape
    block = hidden // 3
    return pl.pallas_call(
        weigh_kernel,
        grid_spec=pltpu.PrefetchScalarGridSpec(
            num_scalar_prefetch=1,
            grid=(3,),
            in_specs=[pl.BlockSpec((16, block, 128), lambda i, o: (0, i, 0))]
            + [pl.BlockSpec((2, block, f.shape[2]), lambda i, o: (0, i, 0)) for f in factors],
            out_specs=pl.BlockSpec((block, 2048), lambda i, o: (i, 0)),
        ),
        out_shape=jax.ShapeDtypeStruct((hidden, 2048), BF16),
        compiler_params=params(),
        name="weigh",
    )(table, spread, *factors)


def starts():
    return [min(PIECE * k, 432 - PIECE) for k in range(NZ)]


def outer_kernel(table_ref, weighted_ref, *refs):
    out_ref, tokens_ref = refs[-2], refs[-1]
    at = 0
    for ref in refs[:-2]:
        tokens_ref[at : at + ref.shape[0]] = ref[...]
        at += ref.shape[0]
    total = jnp.dot(weighted_ref[...], tokens_ref[...], preferred_element_type=F32)
    for k, row in enumerate(starts()):
        out_ref[k] = total[row : row + PIECE, :].astype(out_ref.dtype)


def outer(table, first, weighted, tokens, width, dtype):
    wide = 256
    hidden, depth = weighted.shape
    return pl.pallas_call(
        outer_kernel,
        grid_spec=pltpu.PrefetchScalarGridSpec(
            num_scalar_prefetch=1,
            grid=(width // wide,),
            in_specs=[pl.BlockSpec(weighted.shape, lambda j, c: (0, 0))]
            + [pl.BlockSpec((t.shape[0], wide), lambda j, c: (0, c[first + j])) for t in tokens],
            out_specs=pl.BlockSpec((NZ, PIECE, wide), lambda j, c: (0, 0, j)),
            scratch_shapes=[pltpu.VMEM((depth, wide), BF16)],
        ),
        out_shape=jax.ShapeDtypeStruct((NZ, PIECE, width), dtype),
        compiler_params=params(),
        cost_estimate=pl.CostEstimate(
            flops=2 * hidden * depth * width, bytes_accessed=2 * depth * width + 2 * hidden * depth, transcendentals=0
        ),
        name="outer",
    )(table, weighted, *tokens)


LOW = 27
AWAYS = (0, -1, 1, -2, 2, -3, 3, 4)


def finish_kernel(scale, table_ref, probe_ref, *refs):
    out_ref = refs[-1]
    side, j = pl.program_id(0), pl.program_id(1)
    z = table_ref[LOW - 1]

    def put(ref, away):
        row = jnp.minimum(lax.rem(z + away + NZ, NZ) * PIECE, out_ref.shape[0] - PIECE)
        out_ref[pl.ds(pl.multiple_of(row, 8), PIECE), :] = ref[...].astype(F32)

    for at in range(2):
        pieces = refs[9 * at : 9 * at + 9]

        @pl.when(side == at)
        def _():
            for ref, away in zip(pieces[:7], AWAYS):
                put(ref, away)

        for end in range(2):
            pl.when((side == at) & (j == end))(lambda: put(pieces[7 + end], AWAYS[7]))

    for row in range(0, out_ref.shape[0], 16):
        rows = slice(row, row + 16)
        out_ref[rows, :] = probe_ref[rows, :].astype(F32) * (out_ref[rows, :] * scale)


def finish(table, probe_t, sides, scale):
    hidden, depth = probe_t.shape
    wide = depth // 4
    column = lambda h, j, p: (0, 2 * lax.rem(p[LOW] + h, 2) + j)
    ring = [pl.BlockSpec((PIECE, wide), lambda h, j, p, at=at: (0, jnp.where(h == at, j, 1 - at))) for at in range(2)]
    end = pl.BlockSpec((PIECE, wide), lambda h, j, p: (0, 0))
    return pl.pallas_call(
        lambda *refs: finish_kernel(scale, *refs),
        grid_spec=pltpu.PrefetchScalarGridSpec(
            num_scalar_prefetch=1,
            grid=(2, 2),
            in_specs=[pl.BlockSpec((hidden, wide), column), *([ring[0]] * 7 + [end] * 2 + [ring[1]] * 7 + [end] * 2)],
            out_specs=pl.BlockSpec((hidden, wide), column),
        ),
        out_shape=jax.ShapeDtypeStruct(probe_t.shape, F32),
        compiler_params=params(),
        name="finish",
    )(table, probe_t, *sides[0], *sides[1])


def on_device(tokens, upstream, gate_weight, probe):
    cut, part = lax.axis_index("cuts"), lax.axis_index("fsdp")
    low, z = cut // NZ, cut % NZ
    x, high, core = part // 4, (part // 2) % 2, part % 2
    gate_t, probe_t = gate_weight.T, probe.T
    hidden, depth = gate_t.shape
    rows = tokens.shape[0]

    blocks = ((0, 0), (-1, 0), (1, 0), (0, 1), (2, 0), (-1, 1), (1, 1), (2, 1))
    per_half = depth // 2 // 256
    first = 4
    rest = per_half - first
    away, own = ((1 - low) * per_half, low * per_half)
    table = [((x + dx) % NX) * 4 + (high ^ dy) * 2 + (core ^ flip) for dx, dy in blocks for flip in range(2)]
    table += [side + n for side in (away, own) for n in range(first, per_half)]
    table += [side + n for side in (away, own) for n in range(first)]
    table = jnp.stack([*table, z, low]).astype(jnp.int32)

    turned = upstream.T.reshape(16, hidden, rows)
    mate, left, right = send(tokens, Y_MATE), send(tokens, X_UP), send(tokens, X_DOWN)
    core_tokens = send(tokens, CORE)
    spread = lax.all_to_all(
        turned, AXES, split_axis=0, concat_axis=0, axis_index_groups=REPLICAS, tiled=True
    )
    left, right, mate, table = after((left, right, mate, table), turned)
    beside, across, over = send(mate, X_UP), send(right, X_DOWN), send(right, Y_MATE)
    ring = jnp.concatenate([left, right, mate], 0)
    core_ring = send(ring, CORE)
    near = (tokens, core_tokens, ring, core_ring)
    weight_0 = factor(table, 0, gate_t, probe_t, None, *near)
    beside, across, over = after((beside, across, over), weight_0)
    cuts = (0, 48, 96, rows)
    last = [a[n:m] for a, n, m in zip((beside, over, across), cuts, cuts[1:])]
    beside, across, over = after((beside, across, over), *last)
    last = [send(last[0], X_UP), send(last[1], X_DOWN), send(last[2], Y_MATE)]
    far = jnp.concatenate([across, beside, over], 0)
    core_far = send(far, CORE)
    weight_1 = factor(table, 8, gate_t, probe_t, None, far, core_far)
    last = after(last, weight_1)
    corner = jnp.concatenate(last, 0)
    core_corner = send(corner, CORE)
    weight_2 = factor(table, 14, gate_t, probe_t, None, corner, core_corner)
    weighted = weigh(table, spread, (weight_0, weight_1, weight_2))

    pieces = (tokens, ring, far, corner, core_tokens, core_ring, core_far, core_corner)
    half = rest * 256
    ring_sum = lambda a: lax.all_to_all(
        a, AXES, split_axis=0, concat_axis=0, axis_index_groups=Z_RINGS, tiled=True
    ).astype(F32).sum(0)
    away = outer(table, 16 + 2 * rest, weighted, pieces, first * 256, BF16)
    come = send(away, Y_CUT)
    (table,) = after((table,), away)
    late = outer(table, 16, weighted, pieces, 2 * half, BF16)
    (table,) = after((table,), late)
    own = outer(table, 16 + 2 * rest + first, weighted, pieces, first * 256, F32)
    late = ring_sum(late)
    own = ring_sum((own + come.astype(F32)).astype(BF16))
    late = late[:, half:] + send(late[:, :half].astype(BF16), Y_CUT).astype(F32)
    own = jnp.concatenate([own.astype(BF16), late.astype(BF16)], 1)

    sides = []
    for piece in (own, send(own, Y_CUT)):
        up = down = piece
        gathered = [piece]
        for _ in range(3):
            up, down = send(up, Z_UP), send(down, Z_DOWN)
            gathered += [up, down]
        quarter = depth // 4
        sides.append([*gathered, send(up[:, :quarter], Z_UP), send(down[:, quarter:], Z_DOWN)])
    scale = 1.0 / (rows * lax.axis_size("fsdp") * lax.axis_size("cuts"))
    return finish(table, probe_t, sides, scale).T


def solution(mesh):
    return jax.shard_map(
        on_device,
        mesh=mesh,
        in_specs=(
            P(AXES, None),
            P(AXES, None),
            P(None, "fsdp"),
            P(None, "fsdp"),
        ),
        out_specs=P(None, "fsdp"),
        check_vma=False,
    )
```

```python
import jax
import jax.numpy as jnp
from jax import lax
from jax.experimental import pallas as pl
from jax.experimental.pallas import tpu as pltpu
from jax.sharding import PartitionSpec as P

AXES = ("cuts", "fsdp")
NX, NY, NZ, NC = 4, 4, 8, 2
F32, BF16 = jnp.float32, jnp.bfloat16
VMEM_LIMIT = 62_000_000
VMEM_PART = 28_000_000

PIECE = 56


def device(x, y, z, core):
    return ((y % 2) * NZ + z) * (NX * 2 * NC) + (x * 2 + y // 2) * NC + core


def moves(step):
    chips = [(x, y, z, c) for x in range(NX) for y in range(NY) for z in range(NZ) for c in range(NC)]
    return [(device(*at), device(*step(*at))) for at in chips]


X_UP = moves(lambda x, y, z, c: ((x + 1) % NX, y, z, c))
X_DOWN = moves(lambda x, y, z, c: ((x - 1) % NX, y, z, c))
Z_UP = moves(lambda x, y, z, c: (x, y, (z + 1) % NZ, c))
Z_DOWN = moves(lambda x, y, z, c: (x, y, (z - 1) % NZ, c))
Y_MATE = moves(lambda x, y, z, c: (x, 3 - y, z, c))
Y_CUT = moves(lambda x, y, z, c: (x, y ^ 1, z, c))
CORE = moves(lambda x, y, z, c: (x, y, z, 1 - c))

REPLICAS = [
    [device(x, (low, 3 - low)[high], z, c) for x in range(NX) for high in range(2) for c in range(NC)]
    for low in range(2)
    for z in range(NZ)
]
Z_RINGS = [
    [device(x, y, z, c) for z in range(NZ)] for x in range(NX) for y in range(NY) for c in range(NC)
]


def send(value, pairs):
    return lax.ppermute(value, AXES, pairs)


def after(values, *before):
    return lax.optimization_barrier((*values, *before))[: len(values)]


def params(limit=VMEM_LIMIT):
    return pltpu.CompilerParams(vmem_limit_bytes=limit)


def factor_kernel(weighing, table_ref, gate_ref, probe_ref, *refs):
    tokens_ref, out_ref = refs[-1], refs[-2]
    grads, groups = (refs[:2], refs[2:-2]) if weighing else ((), refs[:-2])
    n = out_ref.shape[2]

    def take(mine_ref, core_ref):
        tokens_ref[:n] = mine_ref[...]
        tokens_ref[n:] = core_ref[...]

    if len(groups) == 2:
        take(*groups)
    else:
        pl.when(pl.program_id(0) == 0)(lambda: take(*groups[:2]))
        pl.when(pl.program_id(0) > 0)(lambda: take(*groups[2:]))
    across = (((1,), (1,)), ((), ()))
    gate = lax.dot_general(gate_ref[...], tokens_ref[...], across, preferred_element_type=F32)
    tangent = lax.dot_general(probe_ref[...], tokens_ref[...], across, preferred_element_type=F32)
    s = 1.0 / (1.0 + jnp.exp(-gate))
    bend = s * (1.0 - s) * (2.0 + gate * (1.0 - 2.0 * s))
    for side in range(2):
        at = slice(side * n, side * n + n)
        if weighing:
            out_ref[side] = (grads[side][0].astype(F32) * bend[:, at] * tangent[:, at]).astype(BF16)
        else:
            out_ref[side] = bend[:, at] * tangent[:, at]


def factor(table, first, gate_t, probe_t, spread, *tokens):
    hidden, depth = gate_t.shape
    rows = 128
    total = sum(t.shape[0] for t in tokens[::2])
    later = int(len(tokens) == 4)
    block = lambda skip: pl.BlockSpec((rows, depth), lambda j, o: (jnp.maximum(j - skip, 0), 0))
    only = pl.BlockSpec((rows, depth), lambda j, o: (0, 0))
    weighing = spread is not None
    return pl.pallas_call(
        lambda *refs: factor_kernel(weighing, *refs),
        grid_spec=pltpu.PrefetchScalarGridSpec(
            num_scalar_prefetch=1,
            grid=(total // rows,),
            in_specs=[pl.BlockSpec((hidden, depth), lambda j, o: (0, 0))] * 2
            + [
                pl.BlockSpec((1, hidden, rows), lambda j, o, side=side: (o[first + 2 * j + side], 0, 0))
                for side in range(2)
            ]
            * weighing
            + [only, only] * later
            + [block(later), block(later)],
            out_specs=pl.BlockSpec((2, hidden, rows), lambda j, o: (0, 0, j)),
            scratch_shapes=[pltpu.VMEM((2 * rows, depth), BF16)],
        ),
        out_shape=jax.ShapeDtypeStruct((2, hidden, total), BF16 if weighing else F32),
        compiler_params=params(VMEM_PART),
        cost_estimate=pl.CostEstimate(flops=0, bytes_accessed=0, transcendentals=0),
        name="factor",
    )(table, gate_t, probe_t, *[spread, spread] * weighing, *tokens)


def weigh(table_ref, grad_ref, factor_refs, out_ref):
    for side in range(2):
        at = 0
        for factor_ref in factor_refs:
            for k in range(0, factor_ref.shape[2], 128):
                grad = grad_ref[table_ref[2 * at + side]].astype(F32)
                to = (side * 8 + at) * 128
                out_ref[:, to : to + 128] = (grad * factor_ref[side, :, k : k + 128]).astype(BF16)
                at += 1


def outer_kernel(table_ref, weighted_ref, *refs):
    out_ref, tokens_ref = refs[-2], refs[-1]
    at = 0
    for ref in refs[:-2]:
        tokens_ref[at : at + ref.shape[0]] = ref[...]
        at += ref.shape[0]
    total = jnp.dot(weighted_ref[...], tokens_ref[...], preferred_element_type=F32)
    for k, row in enumerate(starts()):
        out_ref[k] = total[row : row + PIECE, :].astype(out_ref.dtype)


def weigh_outer_kernel(table_ref, grad_ref, *refs):
    factor_refs, weighted_ref = refs[:3], refs[-3]
    pl.when(pl.program_id(0) == 0)(lambda: weigh(table_ref, grad_ref, factor_refs, weighted_ref))
    outer_kernel(table_ref, weighted_ref, *refs[3:-3], refs[-2], refs[-1])


def starts():
    return [min(PIECE * k, 432 - PIECE) for k in range(NZ)]


def outer(table, first, weighted, tokens, width, dtype, wide):
    whole = lambda a: pl.BlockSpec(a.shape, lambda j, c: (0,) * a.ndim)
    make = isinstance(weighted, tuple)
    operands = weighted if make else (weighted,)
    hidden, depth = operands[0].shape[-2 if make else 0], 2048
    made = [(pl.BlockSpec((hidden, depth), lambda j, c: (0, 0)), jax.ShapeDtypeStruct((hidden, depth), BF16))] * make
    outs = made + [
        (pl.BlockSpec((NZ, PIECE, wide), lambda j, c: (0, 0, j)), jax.ShapeDtypeStruct((NZ, PIECE, width), dtype))
    ]
    return pl.pallas_call(
        weigh_outer_kernel if make else outer_kernel,
        grid_spec=pltpu.PrefetchScalarGridSpec(
            num_scalar_prefetch=1,
            grid=(width // wide,),
            in_specs=[whole(a) for a in operands]
            + [pl.BlockSpec((t.shape[0], wide), lambda j, c: (0, c[first + j])) for t in tokens],
            out_specs=[spec for spec, _ in outs],
            scratch_shapes=[pltpu.VMEM((depth, wide), BF16)],
        ),
        out_shape=[shape for _, shape in outs],
        compiler_params=params(),
        cost_estimate=pl.CostEstimate(
            flops=2 * hidden * depth * width, bytes_accessed=2 * depth * width + 2 * hidden * depth, transcendentals=0
        ),
        name="outer",
    )(table, *operands, *tokens)


LOW = 27
AWAYS = (0, -1, 1, -2, 2, -3, 3, 4)


def finish_kernel(scale, table_ref, probe_ref, *refs):
    out_ref = refs[-1]
    side, j = pl.program_id(0), pl.program_id(1)
    z = table_ref[LOW - 1]

    def put(ref, away):
        row = jnp.minimum(lax.rem(z + away + NZ, NZ) * PIECE, out_ref.shape[0] - PIECE)
        out_ref[pl.ds(pl.multiple_of(row, 8), PIECE), :] = ref[...].astype(F32)

    for at in range(2):
        pieces = refs[9 * at : 9 * at + 9]

        @pl.when(side == at)
        def _():
            for ref, away in zip(pieces[:7], AWAYS):
                put(ref, away)

        for end in range(2):
            pl.when((side == at) & (j == end))(lambda: put(pieces[7 + end], AWAYS[7]))

    for row in range(0, out_ref.shape[0], 16):
        rows = slice(row, row + 16)
        out_ref[rows, :] = probe_ref[rows, :].astype(F32) * (out_ref[rows, :] * scale)


def finish(table, probe_t, sides, scale):
    hidden, depth = probe_t.shape
    wide = depth // 4
    column = lambda h, j, p: (0, 2 * lax.rem(p[LOW] + h, 2) + j)
    ring = [pl.BlockSpec((PIECE, wide), lambda h, j, p, at=at: (0, jnp.where(h == at, j, 1 - at))) for at in range(2)]
    end = pl.BlockSpec((PIECE, wide), lambda h, j, p: (0, 0))
    return pl.pallas_call(
        lambda *refs: finish_kernel(scale, *refs),
        grid_spec=pltpu.PrefetchScalarGridSpec(
            num_scalar_prefetch=1,
            grid=(2, 2),
            in_specs=[pl.BlockSpec((hidden, wide), column), *([ring[0]] * 7 + [end] * 2 + [ring[1]] * 7 + [end] * 2)],
            out_specs=pl.BlockSpec((hidden, wide), column),
        ),
        out_shape=jax.ShapeDtypeStruct(probe_t.shape, F32),
        compiler_params=params(VMEM_PART),
        name="finish",
    )(table, probe_t, *sides[0], *sides[1])


def on_device(tokens, upstream, gate_weight, probe):
    cut, part = lax.axis_index("cuts"), lax.axis_index("fsdp")
    low, z = cut // NZ, cut % NZ
    x, high, core = part // 4, (part // 2) % 2, part % 2
    gate_t, probe_t = gate_weight.T, probe.T
    hidden, depth = gate_t.shape
    rows = tokens.shape[0]

    blocks = ((0, 0), (-1, 0), (1, 0), (0, 1), (2, 0), (-1, 1), (1, 1), (2, 1))
    per_half = depth // 2 // 256
    first = 4
    rest = per_half - first
    away, own = ((1 - low) * per_half, low * per_half)
    table = [((x + dx) % NX) * 4 + (high ^ dy) * 2 + (core ^ flip) for dx, dy in blocks for flip in range(2)]
    table += [side + n for side in (away, own) for n in range(first, per_half)]
    table += [side + n for side in (away, own) for n in range(first)]
    table = jnp.stack([*table, z, low]).astype(jnp.int32)

    turned = upstream.T.reshape(16, hidden, rows)
    mate, left, right = send(tokens, Y_MATE), send(tokens, X_UP), send(tokens, X_DOWN)
    core_tokens = send(tokens, CORE)
    spread = lax.all_to_all(
        turned, AXES, split_axis=0, concat_axis=0, axis_index_groups=REPLICAS, tiled=True
    )
    left, right, mate, table = after((left, right, mate, table), turned)
    beside, across, over = send(mate, X_UP), send(right, X_DOWN), send(right, Y_MATE)
    ring = jnp.concatenate([left, right, mate], 0)
    core_ring = send(ring, CORE)
    near = (tokens, core_tokens, ring, core_ring)
    weight_0 = factor(table, 0, gate_t, probe_t, None, *near)
    beside, across, over = after((beside, across, over), weight_0)
    cuts = (0, 48, 96, rows)
    last = [a[n:m] for a, n, m in zip((beside, over, across), cuts, cuts[1:])]
    beside, across, over = after((beside, across, over), *last)
    last = [send(last[0], X_UP), send(last[1], X_DOWN), send(last[2], Y_MATE)]
    far = jnp.concatenate([across, beside, over], 0)
    core_far = send(far, CORE)
    weight_1 = factor(table, 8, gate_t, probe_t, None, far, core_far)
    last = after(last, weight_1)
    corner = jnp.concatenate(last, 0)
    core_corner = send(corner, CORE)
    weight_2 = factor(table, 14, gate_t, probe_t, None, corner, core_corner)

    pieces = (tokens, ring, far, corner, core_tokens, core_ring, core_far, core_corner)
    half = rest * 256
    ring_sum = lambda a: lax.all_to_all(
        a, AXES, split_axis=0, concat_axis=0, axis_index_groups=Z_RINGS, tiled=True
    ).astype(F32).sum(0)
    weighted, away = outer(
        table, 16 + 2 * rest, (spread, weight_0, weight_1, weight_2), pieces, first * 256, BF16, 256
    )
    come = send(away, Y_CUT)
    (table,) = after((table,), away)
    (late,) = outer(table, 16, weighted, pieces, 2 * half, BF16, 256)
    (table,) = after((table,), late)
    (own,) = outer(table, 16 + 2 * rest + first, weighted, pieces, first * 256, F32, 256)
    late = ring_sum(late)
    own = ring_sum((own + come.astype(F32)).astype(BF16))
    late = late[:, half:] + send(late[:, :half].astype(BF16), Y_CUT).astype(F32)
    own = jnp.concatenate([own.astype(BF16), late.astype(BF16)], 1)

    sides = []
    for piece in (own, send(own, Y_CUT)):
        up = down = piece
        gathered = [piece]
        for _ in range(3):
            up, down = send(up, Z_UP), send(down, Z_DOWN)
            gathered += [up, down]
        quarter = depth // 4
        sides.append([*gathered, send(up[:, :quarter], Z_UP), send(down[:, quarter:], Z_DOWN)])
    scale = 1.0 / (rows * lax.axis_size("fsdp") * lax.axis_size("cuts"))
    return finish(table, probe_t, sides, scale).T


def solution(mesh):
    return jax.shard_map(
        on_device,
        mesh=mesh,
        in_specs=(
            P(AXES, None),
            P(AXES, None),
            P(None, "fsdp"),
            P(None, "fsdp"),
        ),
        out_specs=P(None, "fsdp"),
        check_vma=False,
    )
```

```python
import jax
import jax.numpy as jnp
from jax import lax
from jax.experimental import pallas as pl
from jax.experimental.pallas import tpu as pltpu
from jax.sharding import PartitionSpec as P

AXES = ("cuts", "fsdp")
NX, NY, NZ, NC = 4, 4, 8, 2
F32, BF16 = jnp.float32, jnp.bfloat16
VMEM_LIMIT = 62_000_000
VMEM_PART = 28_000_000

PIECE = 56


def device(x, y, z, core):
    return ((y % 2) * NZ + z) * (NX * 2 * NC) + (x * 2 + y // 2) * NC + core


def moves(step):
    chips = [(x, y, z, c) for x in range(NX) for y in range(NY) for z in range(NZ) for c in range(NC)]
    return [(device(*at), device(*step(*at))) for at in chips]


X_UP = moves(lambda x, y, z, c: ((x + 1) % NX, y, z, c))
X_DOWN = moves(lambda x, y, z, c: ((x - 1) % NX, y, z, c))
Z_UP = moves(lambda x, y, z, c: (x, y, (z + 1) % NZ, c))
Z_DOWN = moves(lambda x, y, z, c: (x, y, (z - 1) % NZ, c))
Z_AWAY = {d: moves(lambda x, y, z, c, d=d: (x, y, (z + d) % NZ, c)) for d in (4, 3, -3, 2, -2, 1, -1)}
Y_MATE = moves(lambda x, y, z, c: (x, 3 - y, z, c))
Y_CUT = moves(lambda x, y, z, c: (x, y ^ 1, z, c))
CORE = moves(lambda x, y, z, c: (x, y, z, 1 - c))

REPLICAS = [
    [device(x, (low, 3 - low)[high], z, c) for x in range(NX) for high in range(2) for c in range(NC)]
    for low in range(2)
    for z in range(NZ)
]
Z_RINGS = [
    [device(x, y, z, c) for z in range(NZ)] for x in range(NX) for y in range(NY) for c in range(NC)
]


def send(value, pairs):
    return lax.ppermute(value, AXES, pairs)


def after(values, *before):
    return lax.optimization_barrier((*values, *before))[: len(values)]


def params(limit=VMEM_LIMIT):
    return pltpu.CompilerParams(vmem_limit_bytes=limit)


def factor_kernel(weighing, table_ref, gate_ref, probe_ref, *refs):
    tokens_ref, out_ref = refs[-1], refs[-2]
    grads, groups = (refs[:2], refs[2:-2]) if weighing else ((), refs[:-2])
    n = out_ref.shape[2]

    def take(mine_ref, core_ref):
        tokens_ref[:n] = mine_ref[...]
        tokens_ref[n:] = core_ref[...]

    if len(groups) == 2:
        take(*groups)
    else:
        pl.when(pl.program_id(0) == 0)(lambda: take(*groups[:2]))
        pl.when(pl.program_id(0) > 0)(lambda: take(*groups[2:]))
    across = (((1,), (1,)), ((), ()))
    gate = lax.dot_general(gate_ref[...], tokens_ref[...], across, preferred_element_type=F32)
    tangent = lax.dot_general(probe_ref[...], tokens_ref[...], across, preferred_element_type=F32)
    s = 1.0 / (1.0 + jnp.exp(-gate))
    bend = s * (1.0 - s) * (2.0 + gate * (1.0 - 2.0 * s))
    for side in range(2):
        at = slice(side * n, side * n + n)
        if weighing:
            out_ref[side] = (grads[side][0].astype(F32) * bend[:, at] * tangent[:, at]).astype(BF16)
        else:
            out_ref[side] = bend[:, at] * tangent[:, at]


def factor(table, first, gate_t, probe_t, spread, *tokens):
    hidden, depth = gate_t.shape
    rows = 128
    total = sum(t.shape[0] for t in tokens[::2])
    later = int(len(tokens) == 4)
    block = lambda skip: pl.BlockSpec((rows, depth), lambda j, o: (jnp.maximum(j - skip, 0), 0))
    only = pl.BlockSpec((rows, depth), lambda j, o: (0, 0))
    weighing = spread is not None
    return pl.pallas_call(
        lambda *refs: factor_kernel(weighing, *refs),
        grid_spec=pltpu.PrefetchScalarGridSpec(
            num_scalar_prefetch=1,
            grid=(total // rows,),
            in_specs=[pl.BlockSpec((hidden, depth), lambda j, o: (0, 0))] * 2
            + [
                pl.BlockSpec((1, hidden, rows), lambda j, o, side=side: (o[first + 2 * j + side], 0, 0))
                for side in range(2)
            ]
            * weighing
            + [only, only] * later
            + [block(later), block(later)],
            out_specs=pl.BlockSpec((2, hidden, rows), lambda j, o: (0, 0, j)),
            scratch_shapes=[pltpu.VMEM((2 * rows, depth), BF16)],
        ),
        out_shape=jax.ShapeDtypeStruct((2, hidden, total), BF16 if weighing else F32),
        compiler_params=params(VMEM_PART),
        cost_estimate=pl.CostEstimate(flops=0, bytes_accessed=0, transcendentals=0),
        name="factor",
    )(table, gate_t, probe_t, *[spread, spread] * weighing, *tokens)


def weigh(table_ref, grad_ref, factor_refs, out_ref):
    for side in range(2):
        at = 0
        for factor_ref in factor_refs:
            for k in range(0, factor_ref.shape[2], 128):
                grad = grad_ref[table_ref[2 * at + side]].astype(F32)
                to = (side * 8 + at) * 128
                out_ref[:, to : to + 128] = (grad * factor_ref[side, :, k : k + 128]).astype(BF16)
                at += 1


def outer_kernel(table_ref, weighted_ref, *refs):
    out_ref, tokens_ref = refs[-2], refs[-1]
    at = 0
    for ref in refs[:-2]:
        tokens_ref[at : at + ref.shape[0]] = ref[...]
        at += ref.shape[0]
    total = jnp.dot(weighted_ref[...], tokens_ref[...], preferred_element_type=F32)
    for k, row in enumerate(starts()):
        out_ref[k] = total[row : row + PIECE, :].astype(out_ref.dtype)


def weigh_outer_kernel(table_ref, grad_ref, *refs):
    factor_refs, weighted_ref = refs[:3], refs[-3]
    pl.when(pl.program_id(0) == 0)(lambda: weigh(table_ref, grad_ref, factor_refs, weighted_ref))
    outer_kernel(table_ref, weighted_ref, *refs[3:-3], refs[-2], refs[-1])


def starts():
    return [min(PIECE * k, 432 - PIECE) for k in range(NZ)]


def outer(table, first, weighted, tokens, width, dtype, wide):
    whole = lambda a: pl.BlockSpec(a.shape, lambda j, c: (0,) * a.ndim)
    make = isinstance(weighted, tuple)
    operands = weighted if make else (weighted,)
    hidden, depth = operands[0].shape[-2 if make else 0], 2048
    made = [(pl.BlockSpec((hidden, depth), lambda j, c: (0, 0)), jax.ShapeDtypeStruct((hidden, depth), BF16))] * make
    outs = made + [
        (pl.BlockSpec((NZ, PIECE, wide), lambda j, c: (0, 0, j)), jax.ShapeDtypeStruct((NZ, PIECE, width), dtype))
    ]
    return pl.pallas_call(
        weigh_outer_kernel if make else outer_kernel,
        grid_spec=pltpu.PrefetchScalarGridSpec(
            num_scalar_prefetch=1,
            grid=(width // wide,),
            in_specs=[whole(a) for a in operands]
            + [pl.BlockSpec((t.shape[0], wide), lambda j, c: (0, c[first + j])) for t in tokens],
            out_specs=[spec for spec, _ in outs],
            scratch_shapes=[pltpu.VMEM((depth, wide), BF16)],
        ),
        out_shape=[shape for _, shape in outs],
        compiler_params=params(),
        cost_estimate=pl.CostEstimate(
            flops=2 * hidden * depth * width, bytes_accessed=2 * depth * width + 2 * hidden * depth, transcendentals=0
        ),
        name="outer",
    )(table, *operands, *tokens)


LOW = 27
AWAYS = (0, -1, 1, -2, 2, -3, 3, 4)


def finish_kernel(scale, table_ref, probe_ref, *refs):
    out_ref = refs[-1]
    side, j = pl.program_id(0), pl.program_id(1)
    z = table_ref[LOW - 1]

    def put(ref, away):
        row = jnp.minimum(lax.rem(z + away + NZ, NZ) * PIECE, out_ref.shape[0] - PIECE)
        out_ref[pl.ds(pl.multiple_of(row, 8), PIECE), :] = ref[...].astype(F32)

    for at in range(2):
        pieces = refs[9 * at : 9 * at + 9]

        @pl.when(side == at)
        def _():
            for ref, away in zip(pieces[:7], AWAYS):
                put(ref, away)

        for end in range(2):
            pl.when((side == at) & (j == end))(lambda: put(pieces[7 + end], AWAYS[7]))

    for row in range(0, out_ref.shape[0], 16):
        rows = slice(row, row + 16)
        out_ref[rows, :] = probe_ref[rows, :].astype(F32) * (out_ref[rows, :] * scale)


def finish(table, probe_t, sides, scale):
    hidden, depth = probe_t.shape
    wide = depth // 4
    column = lambda h, j, p: (0, 2 * lax.rem(p[LOW] + h, 2) + j)
    ring = [pl.BlockSpec((PIECE, wide), lambda h, j, p, at=at: (0, jnp.where(h == at, j, 1 - at))) for at in range(2)]
    end = pl.BlockSpec((PIECE, wide), lambda h, j, p: (0, 0))
    return pl.pallas_call(
        lambda *refs: finish_kernel(scale, *refs),
        grid_spec=pltpu.PrefetchScalarGridSpec(
            num_scalar_prefetch=1,
            grid=(2, 2),
            in_specs=[pl.BlockSpec((hidden, wide), column), *([ring[0]] * 7 + [end] * 2 + [ring[1]] * 7 + [end] * 2)],
            out_specs=pl.BlockSpec((hidden, wide), column),
        ),
        out_shape=jax.ShapeDtypeStruct(probe_t.shape, F32),
        compiler_params=params(VMEM_PART),
        name="finish",
    )(table, probe_t, *sides[0], *sides[1])


def on_device(tokens, upstream, gate_weight, probe):
    cut, part = lax.axis_index("cuts"), lax.axis_index("fsdp")
    low, z = cut // NZ, cut % NZ
    x, high, core = part // 4, (part // 2) % 2, part % 2
    gate_t, probe_t = gate_weight.T, probe.T
    hidden, depth = gate_t.shape
    rows = tokens.shape[0]

    blocks = ((0, 0), (-1, 0), (1, 0), (0, 1), (2, 0), (-1, 1), (1, 1), (2, 1))
    per_half = depth // 2 // 256
    first = 4
    rest = per_half - first
    away, own = ((1 - low) * per_half, low * per_half)
    table = [((x + dx) % NX) * 4 + (high ^ dy) * 2 + (core ^ flip) for dx, dy in blocks for flip in range(2)]
    table += [side + n for side in (away, own) for n in range(first, per_half)]
    table += [side + n for side in (away, own) for n in range(first)]
    table = jnp.stack([*table, z, low]).astype(jnp.int32)

    turned = upstream.T.reshape(16, hidden, rows)
    mate, left, right = send(tokens, Y_MATE), send(tokens, X_UP), send(tokens, X_DOWN)
    core_tokens = send(tokens, CORE)
    spread = lax.all_to_all(
        turned, AXES, split_axis=0, concat_axis=0, axis_index_groups=REPLICAS, tiled=True
    )
    left, right, mate, table = after((left, right, mate, table), turned)
    beside, across, over = send(mate, X_UP), send(right, X_DOWN), send(right, Y_MATE)
    ring = jnp.concatenate([left, right, mate], 0)
    core_ring = send(ring, CORE)
    near = (tokens, core_tokens, ring, core_ring)
    weight_0 = factor(table, 0, gate_t, probe_t, None, *near)
    beside, across, over = after((beside, across, over), weight_0)
    cuts = (0, 48, 96, rows)
    last = [a[n:m] for a, n, m in zip((beside, over, across), cuts, cuts[1:])]
    beside, across, over = after((beside, across, over), *last)
    last = [send(last[0], X_UP), send(last[1], X_DOWN), send(last[2], Y_MATE)]
    far = jnp.concatenate([across, beside, over], 0)
    core_far = send(far, CORE)
    weight_1 = factor(table, 8, gate_t, probe_t, None, far, core_far)
    last = after(last, weight_1)
    corner = jnp.concatenate(last, 0)
    core_corner = send(corner, CORE)
    weight_2 = factor(table, 14, gate_t, probe_t, None, corner, core_corner)

    pieces = (tokens, ring, far, corner, core_tokens, core_ring, core_far, core_corner)
    half = rest * 256
    ring_sum = lambda a: lax.all_to_all(
        a, AXES, split_axis=0, concat_axis=0, axis_index_groups=Z_RINGS, tiled=True
    ).astype(F32).sum(0)
    weighted, away = outer(
        table, 16 + 2 * rest, (spread, weight_0, weight_1, weight_2), pieces, first * 256, BF16, 256
    )
    come = send(away, Y_CUT)
    (table,) = after((table,), away)
    (late,) = outer(table, 16, weighted, pieces, 2 * half, BF16, 256)
    (table,) = after((table,), late)
    (own,) = outer(table, 16 + 2 * rest + first, weighted, pieces, first * 256, F32, 256)
    late = ring_sum(late)
    own = own + come.astype(F32)
    parts = own.astype(BF16)
    take = lambda a, d: lax.dynamic_index_in_dim(a, lax.rem(z + d + NZ, NZ), 0, keepdims=False)
    come = [send(take(parts, d), pairs) for d, pairs in Z_AWAY.items()]
    own = take(own, 0)
    for other in come:
        own = own + other.astype(F32)
    late = late[:, half:] + send(late[:, :half].astype(BF16), Y_CUT).astype(F32)
    own = jnp.concatenate([own.astype(BF16), late.astype(BF16)], 1)

    sides = []
    for piece in (own, send(own, Y_CUT)):
        up = down = piece
        gathered = [piece]
        for _ in range(3):
            up, down = send(up, Z_UP), send(down, Z_DOWN)
            gathered += [up, down]
        quarter = depth // 4
        sides.append([*gathered, send(up[:, :quarter], Z_UP), send(down[:, quarter:], Z_DOWN)])
    scale = 1.0 / (rows * lax.axis_size("fsdp") * lax.axis_size("cuts"))
    return finish(table, probe_t, sides, scale).T


def solution(mesh):
    return jax.shard_map(
        on_device,
        mesh=mesh,
        in_specs=(
            P(AXES, None),
            P(AXES, None),
            P(None, "fsdp"),
            P(None, "fsdp"),
        ),
        out_specs=P(None, "fsdp"),
        check_vma=False,
    )
```

```python
import jax
import jax.numpy as jnp
from jax import lax
from jax.experimental import pallas as pl
from jax.experimental.pallas import tpu as pltpu
from jax.sharding import PartitionSpec as P

AXES = ("cuts", "fsdp")
NX, NY, NZ, NC = 4, 4, 8, 2
F32, BF16 = jnp.float32, jnp.bfloat16
VMEM_LIMIT = 62_000_000
VMEM_PART = 28_000_000

PIECE = 56


def device(x, y, z, core):
    return ((y % 2) * NZ + z) * (NX * 2 * NC) + (x * 2 + y // 2) * NC + core


def moves(step):
    chips = [(x, y, z, c) for x in range(NX) for y in range(NY) for z in range(NZ) for c in range(NC)]
    return [(device(*at), device(*step(*at))) for at in chips]


X_UP = moves(lambda x, y, z, c: ((x + 1) % NX, y, z, c))
X_DOWN = moves(lambda x, y, z, c: ((x - 1) % NX, y, z, c))
Z_UP = moves(lambda x, y, z, c: (x, y, (z + 1) % NZ, c))
Z_DOWN = moves(lambda x, y, z, c: (x, y, (z - 1) % NZ, c))
Z_AWAY = {d: moves(lambda x, y, z, c, d=d: (x, y, (z + d) % NZ, c)) for d in (4, 3, -3, 2, -2, 1, -1)}
Y_MATE = moves(lambda x, y, z, c: (x, 3 - y, z, c))
Y_CUT = moves(lambda x, y, z, c: (x, y ^ 1, z, c))
CORE = moves(lambda x, y, z, c: (x, y, z, 1 - c))

REPLICAS = [
    [device(x, (low, 3 - low)[high], z, c) for x in range(NX) for high in range(2) for c in range(NC)]
    for low in range(2)
    for z in range(NZ)
]
Z_RINGS = [
    [device(x, y, z, c) for z in range(NZ)] for x in range(NX) for y in range(NY) for c in range(NC)
]


def send(value, pairs):
    return lax.ppermute(value, AXES, pairs)


def after(values, *before):
    return lax.optimization_barrier((*values, *before))[: len(values)]


def params(limit=VMEM_LIMIT):
    return pltpu.CompilerParams(vmem_limit_bytes=limit)


def factor_kernel(weighing, table_ref, gate_ref, probe_ref, *refs):
    tokens_ref, out_ref = refs[-1], refs[-2]
    grads, groups = (refs[:2], refs[2:-2]) if weighing else ((), refs[:-2])
    n = out_ref.shape[2]

    def take(mine_ref, core_ref):
        tokens_ref[:n] = mine_ref[...]
        tokens_ref[n:] = core_ref[...]

    if len(groups) == 2:
        take(*groups)
    else:
        pl.when(pl.program_id(0) == 0)(lambda: take(*groups[:2]))
        pl.when(pl.program_id(0) > 0)(lambda: take(*groups[2:]))
    across = (((1,), (1,)), ((), ()))
    gate = lax.dot_general(gate_ref[...], tokens_ref[...], across, preferred_element_type=F32)
    tangent = lax.dot_general(probe_ref[...], tokens_ref[...], across, preferred_element_type=F32)
    s = 1.0 / (1.0 + jnp.exp(-gate))
    bend = s * (1.0 - s) * (2.0 + gate * (1.0 - 2.0 * s))
    for side in range(2):
        at = slice(side * n, side * n + n)
        if weighing:
            out_ref[side] = (grads[side][0].astype(F32) * bend[:, at] * tangent[:, at]).astype(BF16)
        else:
            out_ref[side] = bend[:, at] * tangent[:, at]


def factor(table, first, gate_t, probe_t, spread, *tokens):
    hidden, depth = gate_t.shape
    rows = 128
    total = sum(t.shape[0] for t in tokens[::2])
    later = int(len(tokens) == 4)
    block = lambda skip: pl.BlockSpec((rows, depth), lambda j, o: (jnp.maximum(j - skip, 0), 0))
    only = pl.BlockSpec((rows, depth), lambda j, o: (0, 0))
    weighing = spread is not None
    return pl.pallas_call(
        lambda *refs: factor_kernel(weighing, *refs),
        grid_spec=pltpu.PrefetchScalarGridSpec(
            num_scalar_prefetch=1,
            grid=(total // rows,),
            in_specs=[pl.BlockSpec((hidden, depth), lambda j, o: (0, 0))] * 2
            + [
                pl.BlockSpec((1, hidden, rows), lambda j, o, side=side: (o[first + 2 * j + side], 0, 0))
                for side in range(2)
            ]
            * weighing
            + [only, only] * later
            + [block(later), block(later)],
            out_specs=pl.BlockSpec((2, hidden, rows), lambda j, o: (0, 0, j)),
            scratch_shapes=[pltpu.VMEM((2 * rows, depth), BF16)],
        ),
        out_shape=jax.ShapeDtypeStruct((2, hidden, total), BF16 if weighing else F32),
        compiler_params=params(VMEM_PART),
        cost_estimate=pl.CostEstimate(flops=0, bytes_accessed=0, transcendentals=0),
        name="factor",
    )(table, gate_t, probe_t, *[spread, spread] * weighing, *tokens)


def weigh(table_ref, grad_ref, factor_refs, out_ref):
    for side in range(2):
        at = 0
        for factor_ref in factor_refs:
            for k in range(0, factor_ref.shape[2], 128):
                grad = grad_ref[table_ref[2 * at + side]].astype(F32)
                to = (side * 8 + at) * 128
                out_ref[:, to : to + 128] = (grad * factor_ref[side, :, k : k + 128]).astype(BF16)
                at += 1


def outer_kernel(table_ref, weighted_ref, *refs):
    out_ref, tokens_ref = refs[-2], refs[-1]
    at = 0
    for ref in refs[:-2]:
        tokens_ref[at : at + ref.shape[0]] = ref[...]
        at += ref.shape[0]
    total = jnp.dot(weighted_ref[...], tokens_ref[...], preferred_element_type=F32)
    for k, row in enumerate(starts()):
        out_ref[k] = total[row : row + PIECE, :].astype(out_ref.dtype)


def weigh_outer_kernel(table_ref, grad_ref, *refs):
    factor_refs, weighted_ref = refs[:3], refs[-3]
    pl.when(pl.program_id(0) == 0)(lambda: weigh(table_ref, grad_ref, factor_refs, weighted_ref))
    outer_kernel(table_ref, weighted_ref, *refs[3:-3], refs[-2], refs[-1])


def starts():
    return [min(PIECE * k, 432 - PIECE) for k in range(NZ)]


def outer(table, first, weighted, tokens, width, dtype, wide):
    whole = lambda a: pl.BlockSpec(a.shape, lambda j, c: (0,) * a.ndim)
    make = isinstance(weighted, tuple)
    operands = weighted if make else (weighted,)
    hidden, depth = operands[0].shape[-2 if make else 0], 2048
    made = [(pl.BlockSpec((hidden, depth), lambda j, c: (0, 0)), jax.ShapeDtypeStruct((hidden, depth), BF16))] * make
    outs = made + [
        (pl.BlockSpec((NZ, PIECE, wide), lambda j, c: (0, 0, j)), jax.ShapeDtypeStruct((NZ, PIECE, width), dtype))
    ]
    return pl.pallas_call(
        weigh_outer_kernel if make else outer_kernel,
        grid_spec=pltpu.PrefetchScalarGridSpec(
            num_scalar_prefetch=1,
            grid=(width // wide,),
            in_specs=[whole(a) for a in operands]
            + [pl.BlockSpec((t.shape[0], wide), lambda j, c: (0, c[first + j])) for t in tokens],
            out_specs=[spec for spec, _ in outs],
            scratch_shapes=[pltpu.VMEM((depth, wide), BF16)],
        ),
        out_shape=[shape for _, shape in outs],
        compiler_params=params(),
        cost_estimate=pl.CostEstimate(
            flops=2 * hidden * depth * width, bytes_accessed=2 * depth * width + 2 * hidden * depth, transcendentals=0
        ),
        name="outer",
    )(table, *operands, *tokens)


LOW = 27
AWAYS = (0, -1, 1, -2, 2, -3, 3, 4)


def finish_kernel(scale, table_ref, probe_ref, *refs):
    pieces, out_ref = refs[:9], refs[-1]
    z = table_ref[LOW - 1]

    def put(ref, away):
        row = jnp.minimum(lax.rem(z + away + NZ, NZ) * PIECE, out_ref.shape[0] - PIECE)
        out_ref[pl.ds(pl.multiple_of(row, 8), PIECE), :] = ref[...].astype(F32)

    for ref, away in zip(pieces[:7], AWAYS):
        put(ref, away)
    for end in range(2):
        pl.when(pl.program_id(0) == end)(lambda: put(pieces[7 + end], AWAYS[7]))
    for row in range(0, out_ref.shape[0], 16):
        rows = slice(row, row + 16)
        out_ref[rows, :] = probe_ref[rows, :].astype(F32) * (out_ref[rows, :] * scale)


def finish(table, probe_t, pieces, side, scale, held):
    hidden, depth = probe_t.shape
    wide = depth // 4
    column = pl.BlockSpec((hidden, wide), lambda j, p: (0, 2 * lax.rem(p[LOW] + side, 2) + j))
    ring = pl.BlockSpec((PIECE, wide), lambda j, p: (0, j))
    end = pl.BlockSpec((PIECE, wide), lambda j, p: (0, 0))
    more = [] if held is None else [held]
    return pl.pallas_call(
        lambda *refs: finish_kernel(scale, *refs),
        grid_spec=pltpu.PrefetchScalarGridSpec(
            num_scalar_prefetch=1,
            grid=(2,),
            in_specs=[column, *[ring] * 7, *[end] * 2, *[pl.BlockSpec(memory_space=pl.ANY)] * len(more)],
            out_specs=column,
        ),
        out_shape=jax.ShapeDtypeStruct(probe_t.shape, F32),
        input_output_aliases={11: 0} if more else {},
        compiler_params=params(VMEM_PART),
        name="finish",
    )(table, probe_t, *pieces, *more)


def on_device(tokens, upstream, gate_weight, probe):
    cut, part = lax.axis_index("cuts"), lax.axis_index("fsdp")
    low, z = cut // NZ, cut % NZ
    x, high, core = part // 4, (part // 2) % 2, part % 2
    gate_t, probe_t = gate_weight.T, probe.T
    hidden, depth = gate_t.shape
    rows = tokens.shape[0]

    blocks = ((0, 0), (-1, 0), (1, 0), (0, 1), (2, 0), (-1, 1), (1, 1), (2, 1))
    per_half = depth // 2 // 256
    first = 4
    rest = per_half - first
    away, own = ((1 - low) * per_half, low * per_half)
    table = [((x + dx) % NX) * 4 + (high ^ dy) * 2 + (core ^ flip) for dx, dy in blocks for flip in range(2)]
    table += [side + n for side in (away, own) for n in range(first, per_half)]
    table += [side + n for side in (away, own) for n in range(first)]
    table = jnp.stack([*table, z, low]).astype(jnp.int32)

    turned = upstream.T.reshape(16, hidden, rows)
    mate, left, right = send(tokens, Y_MATE), send(tokens, X_UP), send(tokens, X_DOWN)
    core_tokens = send(tokens, CORE)
    spread = lax.all_to_all(
        turned, AXES, split_axis=0, concat_axis=0, axis_index_groups=REPLICAS, tiled=True
    )
    left, right, mate, table = after((left, right, mate, table), turned)
    beside, across, over = send(mate, X_UP), send(right, X_DOWN), send(right, Y_MATE)
    ring = jnp.concatenate([left, right, mate], 0)
    core_ring = send(ring, CORE)
    near = (tokens, core_tokens, ring, core_ring)
    weight_0 = factor(table, 0, gate_t, probe_t, None, *near)
    beside, across, over = after((beside, across, over), weight_0)
    cuts = (0, 48, 96, rows)
    last = [a[n:m] for a, n, m in zip((beside, over, across), cuts, cuts[1:])]
    beside, across, over = after((beside, across, over), *last)
    last = [send(last[0], X_UP), send(last[1], X_DOWN), send(last[2], Y_MATE)]
    far = jnp.concatenate([across, beside, over], 0)
    core_far = send(far, CORE)
    weight_1 = factor(table, 8, gate_t, probe_t, None, far, core_far)
    last = after(last, weight_1)
    corner = jnp.concatenate(last, 0)
    core_corner = send(corner, CORE)
    weight_2 = factor(table, 14, gate_t, probe_t, None, corner, core_corner)

    pieces = (tokens, ring, far, corner, core_tokens, core_ring, core_far, core_corner)
    half = rest * 256
    ring_sum = lambda a: lax.all_to_all(
        a, AXES, split_axis=0, concat_axis=0, axis_index_groups=Z_RINGS, tiled=True
    ).astype(F32).sum(0)
    weighted, away = outer(
        table, 16 + 2 * rest, (spread, weight_0, weight_1, weight_2), pieces, first * 256, BF16, 256
    )
    come = send(away, Y_CUT)
    (table,) = after((table,), away)
    (late,) = outer(table, 16, weighted, pieces, 2 * half, BF16, 256)
    (table,) = after((table,), late)
    (own,) = outer(table, 16 + 2 * rest + first, weighted, pieces, first * 256, F32, 256)
    late = ring_sum(late)
    def piece(d):
        at = lax.rem(z + d + NZ, NZ)
        mine, other = (lax.dynamic_index_in_dim(a, at, 0, keepdims=False) for a in (own, come))
        return mine + other.astype(F32)

    others = [send(piece(d).astype(BF16), pairs) for d, pairs in Z_AWAY.items()]
    own = piece(0)
    for other in others:
        own = own + other.astype(F32)
    late = late[:, half:] + send(late[:, :half].astype(BF16), Y_CUT).astype(F32)
    own = jnp.concatenate([own.astype(BF16), late.astype(BF16)], 1)

    sides = []
    for piece in (own, send(own, Y_CUT)):
        up = down = piece
        gathered = [piece]
        for _ in range(3):
            up, down = send(up, Z_UP), send(down, Z_DOWN)
            gathered += [up, down]
        quarter = depth // 4
        sides.append([*gathered, send(up[:, :quarter], Z_UP), send(down[:, quarter:], Z_DOWN)])
    scale = 1.0 / (rows * lax.axis_size("fsdp") * lax.axis_size("cuts"))
    held = None
    for side, pieces in enumerate(sides):
        held = finish(table, probe_t, pieces, side, scale, held)
    return held.T


def solution(mesh):
    return jax.shard_map(
        on_device,
        mesh=mesh,
        in_specs=(
            P(AXES, None),
            P(AXES, None),
            P(None, "fsdp"),
            P(None, "fsdp"),
        ),
        out_specs=P(None, "fsdp"),
        check_vma=False,
    )
```

```python
import jax
import jax.numpy as jnp
from jax import lax
from jax.experimental import pallas as pl
from jax.experimental.pallas import tpu as pltpu
from jax.sharding import PartitionSpec as P

AXES = ("cuts", "fsdp")
NX, NY, NZ, NC = 4, 4, 8, 2
F32, BF16 = jnp.float32, jnp.bfloat16
VMEM_LIMIT = 62_000_000
VMEM_PART = 28_000_000

PIECE = 56


def device(x, y, z, core):
    return ((y % 2) * NZ + z) * (NX * 2 * NC) + (x * 2 + y // 2) * NC + core


def moves(step):
    chips = [(x, y, z, c) for x in range(NX) for y in range(NY) for z in range(NZ) for c in range(NC)]
    return [(device(*at), device(*step(*at))) for at in chips]


X_UP = moves(lambda x, y, z, c: ((x + 1) % NX, y, z, c))
X_DOWN = moves(lambda x, y, z, c: ((x - 1) % NX, y, z, c))
Z_UP = moves(lambda x, y, z, c: (x, y, (z + 1) % NZ, c))
Z_DOWN = moves(lambda x, y, z, c: (x, y, (z - 1) % NZ, c))
Z_AWAY = {d: moves(lambda x, y, z, c, d=d: (x, y, (z + d) % NZ, c)) for d in (4, 3, -3, 2, -2, 1, -1)}
Y_MATE = moves(lambda x, y, z, c: (x, 3 - y, z, c))
Y_CUT = moves(lambda x, y, z, c: (x, y ^ 1, z, c))
CORE = moves(lambda x, y, z, c: (x, y, z, 1 - c))

REPLICAS = [
    [device(x, (low, 3 - low)[high], z, c) for x in range(NX) for high in range(2) for c in range(NC)]
    for low in range(2)
    for z in range(NZ)
]
Z_RINGS = [
    [device(x, y, z, c) for z in range(NZ)] for x in range(NX) for y in range(NY) for c in range(NC)
]


def send(value, pairs):
    return lax.ppermute(value, AXES, pairs)


def after(values, *before):
    return lax.optimization_barrier((*values, *before))[: len(values)]


def params(limit=VMEM_LIMIT):
    return pltpu.CompilerParams(vmem_limit_bytes=limit)


def factor_kernel(weighing, table_ref, gate_ref, probe_ref, *refs):
    tokens_ref, out_ref = refs[-1], refs[-2]
    grads, groups = (refs[:2], refs[2:-2]) if weighing else ((), refs[:-2])
    n = out_ref.shape[2]

    def take(mine_ref, core_ref):
        tokens_ref[:n] = mine_ref[...]
        tokens_ref[n:] = core_ref[...]

    if len(groups) == 2:
        take(*groups)
    else:
        pl.when(pl.program_id(0) == 0)(lambda: take(*groups[:2]))
        pl.when(pl.program_id(0) > 0)(lambda: take(*groups[2:]))
    across = (((1,), (1,)), ((), ()))
    gate = lax.dot_general(gate_ref[...], tokens_ref[...], across, preferred_element_type=F32)
    tangent = lax.dot_general(probe_ref[...], tokens_ref[...], across, preferred_element_type=F32)
    s = 1.0 / (1.0 + jnp.exp(-gate))
    bend = s * (1.0 - s) * (2.0 + gate * (1.0 - 2.0 * s))
    for side in range(2):
        at = slice(side * n, side * n + n)
        if weighing:
            out_ref[side] = (grads[side][0].astype(F32) * bend[:, at] * tangent[:, at]).astype(BF16)
        else:
            out_ref[side] = bend[:, at] * tangent[:, at]


def factor(table, first, gate_t, probe_t, spread, *tokens):
    hidden, depth = gate_t.shape
    rows = 128
    total = sum(t.shape[0] for t in tokens[::2])
    later = int(len(tokens) == 4)
    block = lambda skip: pl.BlockSpec((rows, depth), lambda j, o: (jnp.maximum(j - skip, 0), 0))
    only = pl.BlockSpec((rows, depth), lambda j, o: (0, 0))
    weighing = spread is not None
    return pl.pallas_call(
        lambda *refs: factor_kernel(weighing, *refs),
        grid_spec=pltpu.PrefetchScalarGridSpec(
            num_scalar_prefetch=1,
            grid=(total // rows,),
            in_specs=[pl.BlockSpec((hidden, depth), lambda j, o: (0, 0))] * 2
            + [
                pl.BlockSpec((1, hidden, rows), lambda j, o, side=side: (o[first + 2 * j + side], 0, 0))
                for side in range(2)
            ]
            * weighing
            + [only, only] * later
            + [block(later), block(later)],
            out_specs=pl.BlockSpec((2, hidden, rows), lambda j, o: (0, 0, j)),
            scratch_shapes=[pltpu.VMEM((2 * rows, depth), BF16)],
        ),
        out_shape=jax.ShapeDtypeStruct((2, hidden, total), BF16 if weighing else F32),
        compiler_params=params(VMEM_PART),
        cost_estimate=pl.CostEstimate(flops=0, bytes_accessed=0, transcendentals=0),
        name="factor",
    )(table, gate_t, probe_t, *[spread, spread] * weighing, *tokens)


def weigh(table_ref, grad_ref, factor_refs, out_ref):
    for side in range(2):
        at = 0
        for factor_ref in factor_refs:
            for k in range(0, factor_ref.shape[2], 128):
                grad = grad_ref[table_ref[2 * at + side]].astype(F32)
                to = (side * 8 + at) * 128
                out_ref[:, to : to + 128] = (grad * factor_ref[side, :, k : k + 128]).astype(BF16)
                at += 1


def outer_kernel(table_ref, weighted_ref, *refs):
    out_ref, tokens_ref = refs[-2], refs[-1]
    at = 0
    for ref in refs[:-2]:
        tokens_ref[at : at + ref.shape[0]] = ref[...]
        at += ref.shape[0]
    total = jnp.dot(weighted_ref[...], tokens_ref[...], preferred_element_type=F32)
    for k, row in enumerate(starts()):
        out_ref[k] = total[row : row + PIECE, :].astype(out_ref.dtype)


def weigh_outer_kernel(table_ref, grad_ref, *refs):
    factor_refs, weighted_ref = refs[:3], refs[-3]
    pl.when(pl.program_id(0) == 0)(lambda: weigh(table_ref, grad_ref, factor_refs, weighted_ref))
    outer_kernel(table_ref, weighted_ref, *refs[3:-3], refs[-2], refs[-1])


def starts():
    return [min(PIECE * k, 432 - PIECE) for k in range(NZ)]


def outer(table, first, weighted, tokens, width, dtype, wide):
    whole = lambda a: pl.BlockSpec(a.shape, lambda j, c: (0,) * a.ndim)
    make = isinstance(weighted, tuple)
    operands = weighted if make else (weighted,)
    hidden, depth = operands[0].shape[-2 if make else 0], 2048
    made = [(pl.BlockSpec((hidden, depth), lambda j, c: (0, 0)), jax.ShapeDtypeStruct((hidden, depth), BF16))] * make
    outs = made + [
        (pl.BlockSpec((NZ, PIECE, wide), lambda j, c: (0, 0, j)), jax.ShapeDtypeStruct((NZ, PIECE, width), dtype))
    ]
    return pl.pallas_call(
        weigh_outer_kernel if make else outer_kernel,
        grid_spec=pltpu.PrefetchScalarGridSpec(
            num_scalar_prefetch=1,
            grid=(width // wide,),
            in_specs=[whole(a) for a in operands]
            + [pl.BlockSpec((t.shape[0], wide), lambda j, c: (0, c[first + j])) for t in tokens],
            out_specs=[spec for spec, _ in outs],
            scratch_shapes=[pltpu.VMEM((depth, wide), BF16)],
        ),
        out_shape=[shape for _, shape in outs],
        compiler_params=params(),
        cost_estimate=pl.CostEstimate(
            flops=2 * hidden * depth * width, bytes_accessed=2 * depth * width + 2 * hidden * depth, transcendentals=0
        ),
        name="outer",
    )(table, *operands, *tokens)


LOW = 27
AWAYS = (0, -1, 1, -2, 2, -3, 3, 4)


def finish_kernel(scale, table_ref, probe_ref, *refs):
    pieces, out_ref = refs[:9], refs[-1]
    z = table_ref[LOW - 1]

    def put(ref, away):
        row = jnp.minimum(lax.rem(z + away + NZ, NZ) * PIECE, out_ref.shape[0] - PIECE)
        out_ref[pl.ds(pl.multiple_of(row, 8), PIECE), :] = ref[...].astype(F32)

    for ref, away in zip(pieces[:7], AWAYS):
        put(ref, away)
    for end in range(2):
        pl.when(pl.program_id(0) == end)(lambda: put(pieces[7 + end], AWAYS[7]))
    for row in range(0, out_ref.shape[0], 16):
        rows = slice(row, row + 16)
        out_ref[rows, :] = probe_ref[rows, :].astype(F32) * (out_ref[rows, :] * scale)


def finish(table, probe_t, pieces, side, scale, held):
    hidden, depth = probe_t.shape
    wide = depth // 4
    column = pl.BlockSpec((hidden, wide), lambda j, p: (0, 2 * lax.rem(p[LOW] + side, 2) + j))
    ring = pl.BlockSpec((PIECE, wide), lambda j, p: (0, j))
    end = pl.BlockSpec((PIECE, wide), lambda j, p: (0, 0))
    more = [] if held is None else [held]
    return pl.pallas_call(
        lambda *refs: finish_kernel(scale, *refs),
        grid_spec=pltpu.PrefetchScalarGridSpec(
            num_scalar_prefetch=1,
            grid=(2,),
            in_specs=[column, *[ring] * 7, *[end] * 2, *[pl.BlockSpec(memory_space=pl.ANY)] * len(more)],
            out_specs=column,
        ),
        out_shape=jax.ShapeDtypeStruct(probe_t.shape, F32),
        input_output_aliases={11: 0} if more else {},
        compiler_params=params(VMEM_PART),
        name="finish",
    )(table, probe_t, *pieces, *more)


def on_device(tokens, upstream, gate_weight, probe):
    cut, part = lax.axis_index("cuts"), lax.axis_index("fsdp")
    low, z = cut // NZ, cut % NZ
    x, high, core = part // 4, (part // 2) % 2, part % 2
    gate_t, probe_t = gate_weight.T, probe.T
    hidden, depth = gate_t.shape
    rows = tokens.shape[0]

    blocks = ((0, 0), (-1, 0), (1, 0), (0, 1), (2, 0), (-1, 1), (1, 1), (2, 1))
    per_half = depth // 2 // 256
    first = 4
    rest = per_half - first
    away, own = ((1 - low) * per_half, low * per_half)
    table = [((x + dx) % NX) * 4 + (high ^ dy) * 2 + (core ^ flip) for dx, dy in blocks for flip in range(2)]
    table += [side + n for side in (away, own) for n in range(first, per_half)]
    table += [side + n for side in (away, own) for n in range(first)]
    table = jnp.stack([*table, z, low]).astype(jnp.int32)

    turned = upstream.T.reshape(16, hidden, rows)
    mate, left, right = send(tokens, Y_MATE), send(tokens, X_UP), send(tokens, X_DOWN)
    core_tokens = send(tokens, CORE)
    spread = lax.all_to_all(
        turned, AXES, split_axis=0, concat_axis=0, axis_index_groups=REPLICAS, tiled=True
    )
    left, right, mate, table = after((left, right, mate, table), turned)
    beside, across, over = send(mate, X_UP), send(right, X_DOWN), send(right, Y_MATE)
    ring = jnp.concatenate([left, right, mate], 0)
    core_ring = send(ring, CORE)
    near = (tokens, core_tokens, ring, core_ring)
    weight_0 = factor(table, 0, gate_t, probe_t, None, *near)
    beside, across, over = after((beside, across, over), weight_0)
    last = [beside[: rows // 2], over[rows // 2 :]]
    beside, across, over = after((beside, across, over), *last)
    last = [send(last[0], X_UP), send(last[1], X_DOWN)]
    far = jnp.concatenate([across, beside, over], 0)
    core_far = send(far, CORE)
    weight_1 = factor(table, 8, gate_t, probe_t, None, far, core_far)
    last = after(last, weight_1)
    corner = jnp.concatenate(last, 0)
    core_corner = send(corner, CORE)
    weight_2 = factor(table, 14, gate_t, probe_t, None, corner, core_corner)

    pieces = (tokens, ring, far, corner, core_tokens, core_ring, core_far, core_corner)
    half = rest * 256
    ring_sum = lambda a: lax.all_to_all(
        a, AXES, split_axis=0, concat_axis=0, axis_index_groups=Z_RINGS, tiled=True
    ).astype(F32).sum(0)
    weighted, away = outer(
        table, 16 + 2 * rest, (spread, weight_0, weight_1, weight_2), pieces, first * 256, BF16, 256
    )
    come = send(away, Y_CUT)
    (table,) = after((table,), away)
    (late,) = outer(table, 16, weighted, pieces, 2 * half, BF16, 256)
    (table,) = after((table,), late)
    (own,) = outer(table, 16 + 2 * rest + first, weighted, pieces, first * 256, F32, 256)
    late = ring_sum(late)
    def piece(d):
        at = lax.rem(z + d + NZ, NZ)
        mine, other = (lax.dynamic_index_in_dim(a, at, 0, keepdims=False) for a in (own, come))
        return mine + other.astype(F32)

    others = [send(piece(d).astype(BF16), pairs) for d, pairs in Z_AWAY.items()]
    own = piece(0)
    for other in others:
        own = own + other.astype(F32)
    late = late[:, half:] + send(late[:, :half].astype(BF16), Y_CUT).astype(F32)
    own = jnp.concatenate([own.astype(BF16), late.astype(BF16)], 1)

    sides = []
    for piece in (own, send(own, Y_CUT)):
        up = down = piece
        gathered = [piece]
        for _ in range(3):
            up, down = send(up, Z_UP), send(down, Z_DOWN)
            gathered += [up, down]
        quarter = depth // 4
        sides.append([*gathered, send(up[:, :quarter], Z_UP), send(down[:, quarter:], Z_DOWN)])
    scale = 1.0 / (rows * lax.axis_size("fsdp") * lax.axis_size("cuts"))
    held = None
    for side, pieces in enumerate(sides):
        held = finish(table, probe_t, pieces, side, scale, held)
    return held.T


def solution(mesh):
    return jax.shard_map(
        on_device,
        mesh=mesh,
        in_specs=(
            P(AXES, None),
            P(AXES, None),
            P(None, "fsdp"),
            P(None, "fsdp"),
        ),
        out_specs=P(None, "fsdp"),
        check_vma=False,
    )
```
